128 devices in a mesh: row: 8 (over x_lo, y), col: 16 (over z, x_hi, core).
Axes of the slice: x: 4 (x_hi: 2, x_lo: 2; x = x_hi * 2 + x_lo), y: 4, z: 4, core: 2. Of those that a mesh axis runs over, the one named last changes fastest.
Arguments:
- cells: bfloat16 [512, 512, 256], P('row', 'col'), may hold values from -20 to 20
- row_gain: float32 [256], replicated, may hold values from 0.1 to 1.9
- row_qk: bfloat16 [256, 512], replicated, may hold values from -30 to 30
- row_value: bfloat16 [256, 256], replicated, may hold values from -0.375 to 0.375
- row_out: bfloat16 [256, 256], replicated, may hold values from -0.375 to 0.375
- col_gain: float32 [256], replicated, may hold values from 0.1 to 1.9
- col_qk: bfloat16 [256, 512], replicated, may hold values from -30 to 30
- col_value: bfloat16 [256, 256], replicated, may hold values from -0.375 to 0.375
- col_out: bfloat16 [256, 256], replicated, may hold values from -0.375 to 0.375
- mlp_gain: float32 [256], replicated, may hold values from 0.1 to 1.9
- mlp_in: bfloat16 [256, 1024], replicated, may hold values from -0.375 to 0.375
- mlp_out: bfloat16 [1024, 256], replicated, may hold values from -0.1875 to 0.1875
Outputs:
- result: bfloat16 [512, 512, 256], P('row', 'col')
The draws below stay inside these ranges and needn't reach their ends.
All inputs are finite; a program needn't handle non-finite values.
Results may differ from the reference program's by a relative error of at most 0.012.
Values may be sent and summed in bfloat16 or wider, within the bound.
No kernel may reach another device: no remote copies, remote signals or barrier semaphores. Data moves between devices by JAX's collectives and lax.ppermute only.
A program may use at most 64 MiB of HBM per device.

```python
import math
import jax
import jax.numpy as jnp
from jax import lax

C = 256
HEADS = 8
FF = 1024
HS = 32
H = 512
W = 512


def joined_qk(key):
    first, second = jax.random.split(key, 2)
    key_w = jnp.clip(jax.random.normal(first, (C, C), jnp.float32), -6.0, 6.0) * C ** (-0.5)
    free_w = jnp.clip(jax.random.normal(second, (C, C), jnp.float32), -6.0, 6.0) * C ** (-0.5)
    query_w = free_w
    query_w = jnp.clip(query_w, -29.0, 29.0)
    return jnp.concatenate([query_w, key_w], axis=1).astype(jnp.bfloat16)


def draw_cells(key, part):
    key = jax.random.fold_in(key, 5)
    first = jax.random.fold_in(key, 0)
    return jnp.clip(jax.random.normal(first, (H, W, C), jnp.float32), -6.0, 6.0).astype(jnp.bfloat16)


def draw_row_qk(key, part):
    key = jax.random.fold_in(key, 11)
    return joined_qk(key)


def draw_col_qk(key, part):
    key = jax.random.fold_in(key, 23)
    return joined_qk(key)


def bell_draw(rng, shape, width, most, kind=jnp.bfloat16):
    values = jax.random.normal(rng, shape, jnp.float32) * width
    return jnp.minimum(jnp.maximum(values, -most), most).astype(kind)


def setup_inputs(seed: int = 0) -> dict:
    key_list = jax.random.split(jax.random.key(seed), 13)
    return {
        "cells": draw_cells(jax.random.fold_in(key_list[12], 71), 0),
        "row_gain": jnp.clip(1.0 + 0.18 * jax.random.normal(key_list[1], (C,), jnp.float32), 0.1, 1.9),
        "row_qk": draw_row_qk(jax.random.fold_in(key_list[12], 71), 0),
        "row_value": bell_draw(key_list[3], (C, C), C ** -0.5, 0.375),
        "row_out": bell_draw(key_list[4], (C, C), C ** -0.5, 0.375),
        "col_gain": jnp.clip(1.0 + 0.18 * jax.random.normal(key_list[5], (C,), jnp.float32), 0.1, 1.9),
        "col_qk": draw_col_qk(jax.random.fold_in(key_list[12], 71), 0),
        "col_value": bell_draw(key_list[7], (C, C), C ** -0.5, 0.375),
        "col_out": bell_draw(key_list[8], (C, C), C ** -0.5, 0.375),
        "mlp_gain": jnp.clip(1.0 + 0.18 * jax.random.normal(key_list[9], (C,), jnp.float32), 0.1, 1.9),
        "mlp_in": bell_draw(key_list[10], (C, FF), C ** -0.5, 0.375),
        "mlp_out": bell_draw(key_list[11], (FF, C), FF ** -0.5, 0.1875),
    }


def layer_norm(values, gain):
    mean = lax.optimization_barrier(jnp.mean(values, axis=-1, keepdims=True))
    centred = values - mean
    variance = lax.optimization_barrier(jnp.mean(centred * centred, axis=-1, keepdims=True))
    return centred * lax.rsqrt(variance + 1e-05) * gain

def attend_line(line, gain, qk_w, val_w, out_w):
    length = line.shape[0]
    normed = layer_norm(line.astype(jnp.float32), gain).astype(jnp.bfloat16)
    both = jnp.dot(normed, qk_w, preferred_element_type=jnp.float32).astype(jnp.bfloat16)
    values = jnp.dot(normed, val_w, preferred_element_type=jnp.float32).astype(jnp.bfloat16)
    query = both[:, :C].reshape(length, HEADS, HS).astype(jnp.float32)
    keys = both[:, C:].reshape(length, HEADS, HS).astype(jnp.float32)
    vals = values.reshape(length, HEADS, HS).astype(jnp.float32)
    scores = jnp.einsum('qhd,khd->hqk', query, keys) / math.sqrt(HS)
    prob = jax.nn.softmax(scores, axis=-1).astype(jnp.bfloat16)
    mixed = jnp.einsum('hqk,khd->qhd', prob.astype(jnp.float32), vals).reshape(length, C).astype(jnp.bfloat16)
    return (line.astype(jnp.float32) + jnp.dot(mixed, out_w, preferred_element_type=jnp.float32)).astype(jnp.bfloat16)

def mlp_line(line, gain, w_first, w_second):
    normed = layer_norm(line.astype(jnp.float32), gain).astype(jnp.bfloat16)
    hidden = jax.nn.gelu(jnp.dot(normed, w_first, preferred_element_type=jnp.float32), approximate=True).astype(jnp.bfloat16)
    return (line.astype(jnp.float32) + jnp.dot(hidden, w_second, preferred_element_type=jnp.float32)).astype(jnp.bfloat16)

def reference(cells, row_gain, row_qk, row_value, row_out, col_gain, col_qk, col_value, col_out, mlp_gain, mlp_in, mlp_out):
    after_rows = lax.map(lambda line: attend_line(line, row_gain, row_qk, row_value, row_out), cells)
    turned = jnp.swapaxes(after_rows, 0, 1)
    after_cols = jnp.swapaxes(lax.map(lambda line: attend_line(line, col_gain, col_qk, col_value, col_out), turned), 0, 1)
    return lax.map(lambda line: mlp_line(line, mlp_gain, mlp_in, mlp_out), after_cols)
```

```python
import math

import jax
import jax.numpy as jnp
from jax import lax
from jax.experimental import pallas as pl
from jax.experimental.pallas import tpu as pltpu
from jax.sharding import PartitionSpec as P

HEADS = 8
HEAD = 32
WIDTH = 256
LINE = 512
LINES = 4
FF = 1024
HALF = 128
GROUPS = 2
IN_GROUP = 4
BLOCK = 256
SCALE = math.log2(math.e) / math.sqrt(HEAD)
GELU_A = math.sqrt(2.0 / math.pi)
GELU_B = GELU_A * 0.044715


def layer_norm(values, gain):
    mean = jnp.mean(values, axis=-1, keepdims=True)
    centred = values - mean
    variance = jnp.mean(centred * centred, axis=-1, keepdims=True)
    return centred * lax.rsqrt(variance + 1e-05) * gain


def matmul(left, right):
    return jnp.dot(left, right, preferred_element_type=jnp.float32)


def fill_ones(mixer):
    lane = lax.broadcasted_iota(jnp.int32, (LINE, HALF), 1) // HEAD
    for group in range(GROUPS):
        for head in range(IN_GROUP):
            ones = jnp.where(lane == head, 1.0, 0.0).astype(jnp.bfloat16)
            mixer[group, head * LINE : (head + 1) * LINE, HALF:] = ones


def attend(line, gain, qk_w, val_w, out_w, mixer, probs):
    normed = layer_norm(line, gain).astype(jnp.bfloat16)
    both = matmul(normed, qk_w)
    values = matmul(normed, val_w).astype(jnp.bfloat16)
    query = both[:, :WIDTH].astype(jnp.bfloat16).astype(jnp.float32) * SCALE
    query_hi = query.astype(jnp.bfloat16)
    query_lo = (query - query_hi.astype(jnp.float32)).astype(jnp.bfloat16)
    keys = both[:, WIDTH:].astype(jnp.bfloat16)
    lane = lax.broadcasted_iota(jnp.int32, (LINE, HALF), 1) // HEAD
    mixed = []
    for group in range(GROUPS):
        lanes = slice(group * HALF, (group + 1) * HALF)
        group_query = jnp.concatenate([query_hi[:, lanes], query_lo[:, lanes]], axis=1)
        group_keys = keys[:, lanes]
        group_values = values[:, lanes]
        zero = jnp.zeros_like(group_keys)
        for head in range(IN_GROUP):
            rows = slice(head * LINE, (head + 1) * LINE)
            head_keys = jnp.where(lane == head, group_keys, zero)
            head_keys = jnp.concatenate([head_keys, head_keys], axis=1)
            mixer[group, rows, :HALF] = jnp.where(lane == head, group_values, zero)
            for start in range(0, LINE, BLOCK):
                scores = lax.dot_general(
                    group_query[start : start + BLOCK],
                    head_keys,
                    (((1,), (1,)), ((), ())),
                    preferred_element_type=jnp.float32,
                )
                scores = scores - jnp.max(scores, axis=-1, keepdims=True)
                probs[start : start + BLOCK, rows] = jnp.exp2(scores).astype(jnp.bfloat16)
        sums = matmul(probs[...], mixer[group])
        mixed.append((sums[:, :HALF] / sums[:, HALF:]).astype(jnp.bfloat16))
    return line + matmul(jnp.concatenate(mixed, axis=1), out_w)


def row_kernel(cells, gain, qk_w, val_w, out_w, out, mixer, probs, turned):
    step = pl.program_id(0)

    @pl.when(step == 0)
    def _():
        fill_ones(mixer)

    line = cells[:, 0].reshape(LINE, WIDTH).astype(jnp.float32)
    done = attend(line, gain[...], qk_w[...], val_w[...], out_w[...], mixer, probs)
    for lanes in range(GROUPS):
        turned[lanes, pl.ds(step, LINE, stride=LINES), :] = done[:, lanes * HALF : (lanes + 1) * HALF]

    @pl.when(step == LINES - 1)
    def _():
        n_row, n_col, deep = out.shape[:3]
        for lanes in range(GROUPS):
            here = slice(lanes * HALF, (lanes + 1) * HALF)
            blocks = turned[lanes].astype(jnp.bfloat16).reshape(n_col, n_row, deep, HALF)
            for r in range(n_row):
                out[r, :, :, here] = blocks[:, r]


def col_kernel(
    cells, gain, qk_w, val_w, out_w, mlp_gain, mlp_in, mlp_out, out, mixer, probs, turned
):
    step = pl.program_id(0)

    @pl.when(step == 0)
    def _():
        fill_ones(mixer)
        for lanes in range(GROUPS):
            turned[lanes] = cells[:, lanes * HALF : (lanes + 1) * HALF].astype(jnp.float32)

    parts = LINE // LINES
    line = jnp.concatenate(
        [
            jnp.concatenate(
                [
                    turned[lanes, pl.ds(step * LINES + j, parts, stride=LINES * LINES), :]
                    for lanes in range(GROUPS)
                ],
                axis=1,
            )
            for j in range(LINES)
        ],
        axis=0,
    )
    done = attend(line, gain[...], qk_w[...], val_w[...], out_w[...], mixer, probs)
    cols = done.astype(jnp.bfloat16).astype(jnp.float32)
    normed = layer_norm(cols, mlp_gain[...]).astype(jnp.bfloat16)
    pre = matmul(normed, mlp_in[...])
    inner = jnp.tanh(pre * (GELU_A + GELU_B * (pre * pre)))
    hidden = (pre * (0.5 + 0.5 * inner)).astype(jnp.bfloat16)
    result = (cols + matmul(hidden, mlp_out[...])).astype(jnp.bfloat16)
    own = out.shape[0]
    deep = parts // own
    for j in range(LINES):
        part = result[j * parts : (j + 1) * parts].reshape(own, deep, WIDTH)
        out[:, 0, j * deep : (j + 1) * deep, :] = part


def join_kernel(blocks, out, turned):
    n_row = blocks.shape[0]
    rows, cols = out.shape[0], out.shape[1]
    deep = rows // LINES
    for lanes in range(GROUPS):
        here = slice(lanes * HALF, (lanes + 1) * HALF)
        for r in range(n_row):
            for m in range(LINES):
                for j in range(LINES):
                    turned[lanes, pl.ds(j * cols + LINES * r + m, deep, stride=LINES * cols), :] = blocks[
                        r, m, j * deep : (j + 1) * deep, here
                    ].astype(jnp.float32)
    for lanes in range(GROUPS):
        here = slice(lanes * HALF, (lanes + 1) * HALF)
        out[:, :, here] = turned[lanes].astype(jnp.bfloat16).reshape(rows, cols, HALF)


def whole(array):
    return pl.BlockSpec(array.shape, lambda step: (0,) * array.ndim)


def attend_scratch():
    return [
        pltpu.VMEM((GROUPS, IN_GROUP * LINE, WIDTH), jnp.bfloat16),
        pltpu.VMEM((LINE, IN_GROUP * LINE), jnp.bfloat16),
        pltpu.VMEM((GROUPS, LINES * LINE, HALF), jnp.float32),
    ]


def params():
    return pltpu.CompilerParams(vmem_limit_bytes=48 * 2**20)


def row_attention(strips, n_row, *weights):
    n_col, lines, cols, width = strips.shape
    shape = (n_row, n_col, LINES * LINES, width)
    return pl.pallas_call(
        row_kernel,
        grid=(lines,),
        in_specs=[pl.BlockSpec((n_col, 1, cols, width), lambda step: (0, step, 0, 0))]
        + [whole(weight) for weight in weights],
        out_specs=pl.BlockSpec(shape, lambda step: (0, 0, 0, 0)),
        out_shape=jax.ShapeDtypeStruct(shape, jnp.bfloat16),
        scratch_shapes=attend_scratch(),
        compiler_params=params(),
        name="row_attention",
    )(strips, *weights)


def col_attention(cells, n_row, *weights):
    rows = LINE // n_row
    return pl.pallas_call(
        col_kernel,
        grid=(LINES,),
        in_specs=[whole(cells)] + [whole(weight) for weight in weights],
        out_specs=pl.BlockSpec((n_row, 1, rows, WIDTH), lambda step: (0, step, 0, 0)),
        out_shape=jax.ShapeDtypeStruct((n_row, LINES, rows, WIDTH), jnp.bfloat16),
        scratch_shapes=attend_scratch(),
        compiler_params=params(),
        name="col_attention_mlp",
    )(cells, *weights)


def join(blocks, rows, cols):
    return pl.pallas_call(
        join_kernel,
        out_shape=jax.ShapeDtypeStruct((rows, cols, WIDTH), jnp.bfloat16),
        scratch_shapes=[pltpu.VMEM((GROUPS, LINES * LINE, HALF), jnp.float32)],
        compiler_params=params(),
        name="join_blocks",
    )(blocks)


def per_device(
    cells,
    row_gain,
    row_qk,
    row_value,
    row_out,
    col_gain,
    col_qk,
    col_value,
    col_out,
    mlp_gain,
    mlp_in,
    mlp_out,
):
    n_row = lax.axis_size("row")
    n_col = lax.axis_size("col")
    rows, cols, width = cells.shape
    row_gain, col_gain, mlp_gain = (g.reshape(1, width) for g in (row_gain, col_gain, mlp_gain))
    strips = lax.all_to_all(cells, "col", split_axis=0, concat_axis=0, tiled=True)
    strips = strips.reshape(n_col, rows // n_col, cols, width)
    after_rows = row_attention(strips, n_row, row_gain, row_qk, row_value, row_out)
    columns = lax.all_to_all(
        after_rows.reshape(-1, width), ("row", "col"), split_axis=0, concat_axis=0, tiled=True
    )
    finished = col_attention(
        columns, n_row, col_gain, col_qk, col_value, col_out, mlp_gain, mlp_in, mlp_out
    )
    blocks = lax.all_to_all(
        finished.reshape(-1, width), "row", split_axis=0, concat_axis=0, tiled=True
    )
    return join(blocks.reshape(n_row, LINES, rows, width), rows, cols)


def solution(mesh):
    in_specs = (P("row", "col", None), P(), P(), P(), P(), P(), P(), P(), P(), P(), P(), P())
    out_specs = P("row", "col", None)
    return jax.shard_map(
        per_device, mesh=mesh, in_specs=in_specs, out_specs=out_specs, check_vma=False
    )
```

```python
import math

import jax
import jax.numpy as jnp
from jax import lax
from jax.experimental import pallas as pl
from jax.experimental.pallas import tpu as pltpu
from jax.sharding import PartitionSpec as P

HEADS = 8
HEAD = 32
WIDTH = 256
LINE = 512
LINES = 4
HALF = 128
GROUPS = 2
IN_GROUP = 4
BLOCK = 256
SCALE = math.log2(math.e) / math.sqrt(HEAD)
GELU_A = math.sqrt(2.0 / math.pi)
GELU_B = GELU_A * 0.044715


def layer_norm(values, gain):
    mean = jnp.mean(values, axis=-1, keepdims=True)
    centred = values - mean
    variance = jnp.mean(centred * centred, axis=-1, keepdims=True)
    return centred * lax.rsqrt(variance + 1e-05) * gain


def matmul(left, right):
    return jnp.dot(left, right, preferred_element_type=jnp.float32)


def fill_ones(mixer):
    lane = lax.broadcasted_iota(jnp.int32, (LINE, HALF), 1) // HEAD
    for group in range(GROUPS):
        for head in range(IN_GROUP):
            ones = jnp.where(lane == head, 1.0, 0.0).astype(jnp.bfloat16)
            mixer[group, head * LINE : (head + 1) * LINE, HALF:] = ones


class Line:
    def __init__(self, load, store, gain, qk_w, val_w, out_w, mixer, probs):
        self.load, self.store = load, store
        self.gain, self.qk_w, self.val_w, self.out_w = gain, qk_w, val_w, out_w
        self.mixer, self.probs = mixer, probs
        self.mixed = []

    def project(self):
        normed = layer_norm(self.load(), self.gain[...]).astype(jnp.bfloat16)
        both = matmul(normed, self.qk_w[...])
        self.values = matmul(normed, self.val_w[...]).astype(jnp.bfloat16)
        query = both[:, :WIDTH].astype(jnp.bfloat16).astype(jnp.float32) * SCALE
        self.query_hi = query.astype(jnp.bfloat16)
        self.query_lo = (query - self.query_hi.astype(jnp.float32)).astype(jnp.bfloat16)
        self.keys = both[:, WIDTH:].astype(jnp.bfloat16)

    def weigh(self, group):
        lanes = slice(group * HALF, (group + 1) * HALF)
        query = jnp.concatenate([self.query_hi[:, lanes], self.query_lo[:, lanes]], axis=1)
        keys = self.keys[:, lanes]
        values = self.values[:, lanes]
        zero = jnp.zeros_like(keys)
        lane = lax.broadcasted_iota(jnp.int32, (LINE, HALF), 1) // HEAD
        for head in range(IN_GROUP):
            rows = slice(head * LINE, (head + 1) * LINE)
            self.mixer[group, rows, :HALF] = jnp.where(lane == head, values, zero)
            head_keys = jnp.where(lane == head, keys, zero)
            head_keys = jnp.concatenate([head_keys, head_keys], axis=1)
            for start in range(0, LINE, BLOCK):
                scores = lax.dot_general(
                    query[start : start + BLOCK],
                    head_keys,
                    (((1,), (1,)), ((), ())),
                    preferred_element_type=jnp.float32,
                )
                scores = scores - jnp.max(scores, axis=-1, keepdims=True)
                self.probs[group, start : start + BLOCK, rows] = jnp.exp2(scores).astype(jnp.bfloat16)

    def mix(self, group):
        sums = matmul(self.probs[group], self.mixer[group])
        self.mixed.append((sums[:, :HALF] / sums[:, HALF:]).astype(jnp.bfloat16))

    def finish(self):
        self.store(self.load() + matmul(jnp.concatenate(self.mixed, axis=1), self.out_w[...]))


def attend(lines):
    lines[0].project()
    lines[0].weigh(0)
    for line, later in zip(lines, lines[1:] + [None]):
        line.mix(0)
        line.weigh(1)
        if later is not None:
            later.project()
        line.mix(1)
        if later is not None:
            later.weigh(0)
        line.finish()


def row_kernel(
    cells, gain, qk_w, val_w, out_w, later_gain, last_gain, out, later_out, last_out, mixer, probs, turned
):
    fill_ones(mixer)
    later_out[...] = later_gain[...]
    last_out[...] = last_gain[...]

    def line(j):
        def load():
            return cells[:, j].reshape(LINE, WIDTH).astype(jnp.float32)

        def store(done):
            for lanes in range(GROUPS):
                turned[lanes, pl.ds(j, LINE, stride=LINES), :] = done[:, lanes * HALF : (lanes + 1) * HALF]

        return Line(load, store, gain, qk_w, val_w, out_w, mixer, probs)

    attend([line(j) for j in range(LINES)])
    n_row, n_col, deep = out.shape[:3]
    for lanes in range(GROUPS):
        here = slice(lanes * HALF, (lanes + 1) * HALF)
        blocks = turned[lanes].astype(jnp.bfloat16).reshape(n_col, n_row, deep, HALF)
        for r in range(n_row):
            out[r, :, :, here] = blocks[:, r]


def col_kernel(cells, gain, qk_w, val_w, out_w, out, mixer, probs):
    fill_ones(mixer)

    def line(m):
        def load():
            tiles = cells[...].reshape(LINE // LINES, LINES * LINES, WIDTH)[:, m // 2 * 8 : m // 2 * 8 + 8]
            tiles = tiles.astype(jnp.float32).reshape(LINE // 8, 2, 8, WIDTH)
            even, odd = tiles[:, 0], tiles[:, 1]
            if m % 2:
                even = pltpu.roll(even, LINES, 1)
            else:
                odd = pltpu.roll(odd, LINES, 1)
            row = lax.broadcasted_iota(jnp.int32, even.shape, 1)
            return jnp.where(row < LINES, even, odd).reshape(LINE, WIDTH)

        def store(done):
            out[:, m] = done.astype(jnp.bfloat16).reshape(out.shape[0], out.shape[2], WIDTH)

        return Line(load, store, gain, qk_w, val_w, out_w, mixer, probs)

    attend([line(m) for m in range(LINES)])


def mlp_kernel(blocks, gain, in_w, out_w, out, swap, done, sems):
    rows, cols = out.shape[:2]
    deep = rows // LINES
    cells = deep * cols
    to = lax.broadcasted_iota(jnp.int32, (cells, cells), 0)
    come = lax.broadcasted_iota(jnp.int32, (cells, cells), 1)
    moved = come == to % cols * deep + to // cols
    swap[...] = jnp.where(moved, 1.0, 0.0).astype(jnp.bfloat16)
    copies = []
    for part in range(LINES):
        here = slice(part * deep, (part + 1) * deep)
        line = matmul(swap[...], blocks[:, :, here].reshape(cells, WIDTH))
        normed = layer_norm(line, gain[...]).astype(jnp.bfloat16)
        for start in range(0, cells, BLOCK):
            pre = matmul(normed[start : start + BLOCK], in_w[...])
            inner = jnp.tanh(pre * (GELU_A + GELU_B * (pre * pre)))
            hidden = (pre * (0.5 + 0.5 * inner)).astype(jnp.bfloat16)
            result = line[start : start + BLOCK] + matmul(hidden, out_w[...])
            first = part * deep + start // cols
            done[first : first + BLOCK // cols] = result.astype(jnp.bfloat16).reshape(
                BLOCK // cols, cols, WIDTH
            )
        copies.append(pltpu.make_async_copy(done.at[here], out.at[here], sems.at[part]))
        copies[-1].start()
    for copy in copies:
        copy.wait()


IN_VMEM = pl.BlockSpec(memory_space=pltpu.VMEM)
PARAMS = pltpu.CompilerParams(vmem_limit_bytes=40 * 2**20)


def bf16(*shape):
    return jax.ShapeDtypeStruct(shape, jnp.bfloat16)


def attend_scratch():
    return [
        pltpu.VMEM((GROUPS, IN_GROUP * LINE, WIDTH), jnp.bfloat16),
        pltpu.VMEM((GROUPS, LINE, IN_GROUP * LINE), jnp.bfloat16),
    ]


def row_attention(n_row, strips, gain, qk_w, val_w, out_w, *gains):
    n_col = strips.shape[0]
    return pl.pallas_call(
        row_kernel,
        in_specs=[IN_VMEM] * 7,
        out_specs=[IN_VMEM] * 3,
        out_shape=[bf16(n_row, n_col, LINES * LINES, WIDTH)]
        + [jax.ShapeDtypeStruct(later.shape, later.dtype) for later in gains],
        scratch_shapes=attend_scratch() + [pltpu.VMEM((GROUPS, LINES * LINE, HALF), jnp.float32)],
        compiler_params=PARAMS,
        name="row_attention",
    )(strips, gain, qk_w, val_w, out_w, *gains)


def col_attention(n_row, columns, *weights):
    return pl.pallas_call(
        col_kernel,
        in_specs=[IN_VMEM] * 5,
        out_specs=IN_VMEM,
        out_shape=bf16(n_row, LINES, LINE // n_row, WIDTH),
        scratch_shapes=attend_scratch(),
        compiler_params=PARAMS,
        name="col_attention",
    )(columns, *weights)


def mlp(cols, blocks, *weights):
    rows = blocks.shape[2]
    cells = rows // LINES * cols
    return pl.pallas_call(
        mlp_kernel,
        in_specs=[IN_VMEM] * 4,
        out_specs=pl.BlockSpec(memory_space=pl.ANY),
        out_shape=bf16(rows, cols, WIDTH),
        scratch_shapes=[
            pltpu.VMEM((cells, cells), jnp.bfloat16),
            pltpu.VMEM((rows, cols, WIDTH), jnp.bfloat16),
            pltpu.SemaphoreType.DMA((LINES,)),
        ],
        compiler_params=PARAMS,
        name="mlp",
    )(blocks, *weights)


def per_device(
    cells,
    row_gain,
    row_qk,
    row_value,
    row_out,
    col_gain,
    col_qk,
    col_value,
    col_out,
    mlp_gain,
    mlp_in,
    mlp_out,
):
    n_row = lax.axis_size("row")
    n_col = lax.axis_size("col")
    rows, cols, width = cells.shape
    row_gain, col_gain, mlp_gain = (g.reshape(1, width) for g in (row_gain, col_gain, mlp_gain))
    strips = lax.all_to_all(cells, "col", split_axis=0, concat_axis=0, tiled=True)
    strips = strips.reshape(n_col, LINES, cols, width)
    after_rows, col_gain, mlp_gain = row_attention(
        n_row, strips, row_gain, row_qk, row_value, row_out, col_gain, mlp_gain
    )
    columns = lax.all_to_all(
        after_rows.reshape(-1, width), ("row", "col"), split_axis=0, concat_axis=0, tiled=True
    )
    after_cols = col_attention(n_row, columns, col_gain, col_qk, col_value, col_out)
    blocks = lax.all_to_all(
        after_cols.reshape(-1, width), "row", split_axis=0, concat_axis=0, tiled=True
    )
    return mlp(cols, blocks.reshape(n_row, LINES, rows, width), mlp_gain, mlp_in, mlp_out)


def solution(mesh):
    in_specs = (P("row", "col", None), P(), P(), P(), P(), P(), P(), P(), P(), P(), P(), P())
    out_specs = P("row", "col", None)
    return jax.shard_map(
        per_device, mesh=mesh, in_specs=in_specs, out_specs=out_specs, check_vma=False
    )
```

```python
import functools
import math

import jax
import jax.numpy as jnp
from jax import lax
from jax.experimental import pallas as pl
from jax.experimental.pallas import tpu as pltpu
from jax.sharding import PartitionSpec as P

HEADS = 8
HEAD = 32
WIDTH = 256
LINE = 512
LINES = 4
HALF = 128
GROUPS = 2
IN_GROUP = 4
BLOCK = 256
CHUNK = 256
SCALE = math.log2(math.e) / math.sqrt(HEAD)
GELU_A = math.sqrt(2.0 / math.pi)
GELU_B = GELU_A * 0.044715


def layer_norm(values, gain):
    mean = jnp.mean(values, axis=-1, keepdims=True)
    centred = values - mean
    variance = jnp.mean(centred * centred, axis=-1, keepdims=True)
    return centred * lax.rsqrt(variance + 1e-05) * gain


def matmul(left, right):
    return jnp.dot(left, right, preferred_element_type=jnp.float32)


def dot(left, right, left_dim, right_dim):
    return lax.dot_general(
        left, right, (((left_dim,), (right_dim,)), ((), ())), preferred_element_type=jnp.float32
    )


class Line:
    def __init__(self, load, store, gain, qk_w, val_w, out_w, probs):
        self.load, self.store = load, store
        self.gain, self.qk_w, self.val_w, self.out_w = gain, qk_w, val_w, out_w
        self.probs = probs
        self.largest = {}
        self.mixed = []

    def project(self):
        normed = layer_norm(self.load(), self.gain[...]).astype(jnp.bfloat16)
        both = matmul(normed, self.qk_w[...])
        self.values = dot(self.val_w[...], normed, 0, 1).astype(jnp.bfloat16)
        query = both[:, :WIDTH].astype(jnp.bfloat16).astype(jnp.float32) * SCALE
        self.query_hi = query.astype(jnp.bfloat16)
        self.query_lo = (query - self.query_hi.astype(jnp.float32)).astype(jnp.bfloat16)
        self.keys = both[:, WIDTH:].astype(jnp.bfloat16)

    def weigh(self, group):
        lanes = slice(group * HALF, (group + 1) * HALF)
        query = jnp.concatenate([self.query_hi[:, lanes], self.query_lo[:, lanes]], axis=1)
        keys = self.keys[:, lanes]
        zero = jnp.zeros_like(keys)
        lane = lax.broadcasted_iota(jnp.int32, (LINE, HALF), 1) // HEAD
        for head in range(IN_GROUP):
            head_keys = jnp.where(lane == head, keys, zero)
            head_keys = jnp.concatenate([head_keys, head_keys], axis=1)
            for start in range(0, LINE, BLOCK):
                here = slice(start, start + BLOCK)
                for chunk in range(0, LINE, CHUNK):
                    rows = slice(chunk, chunk + CHUNK)
                    scores = dot(head_keys[rows], query[here], 1, 1)
                    largest = jnp.max(scores, axis=0, keepdims=True)
                    self.largest[group, head, chunk, start] = largest
                    weights = jnp.exp2(scores - largest).astype(jnp.bfloat16)
                    self.probs[group * IN_GROUP + head, rows, here] = weights

    def mix(self, group):
        ones = jnp.ones((16, LINE), jnp.bfloat16)
        for head in range(IN_GROUP):
            index = group * IN_GROUP + head
            values = jnp.concatenate([self.values[index * HEAD : (index + 1) * HEAD], ones], axis=0)
            chunks = range(0, LINE, CHUNK)
            scales = [
                jnp.concatenate(
                    [self.largest[group, head, chunk, start] for start in range(0, LINE, BLOCK)], axis=1
                )
                for chunk in chunks
            ]
            largest = functools.reduce(jnp.maximum, scales)
            total = 0.0
            for chunk, scale in zip(chunks, scales):
                rows = slice(chunk, chunk + CHUNK)
                total += matmul(values[:, rows], self.probs[index, rows]) * jnp.exp2(scale - largest)
            self.mixed.append((total[:HEAD] / total[HEAD : HEAD + 1]).astype(jnp.bfloat16))

    def finish(self):
        self.store(self.load() + dot(jnp.concatenate(self.mixed, axis=0), self.out_w[...], 0, 0))


def attend(lines):
    lines[0].project()
    lines[0].weigh(0)
    for line, later in zip(lines, lines[1:] + [None]):
        line.mix(0)
        line.weigh(1)
        if later is not None:
            later.project()
        line.mix(1)
        if later is not None:
            later.weigh(0)
        line.finish()


def row_kernel(
    cells, gain, qk_w, val_w, out_w, later_gain, last_gain, out, later_out, last_out, probs, turned
):
    later_out[...] = later_gain[...]
    last_out[...] = last_gain[...]

    def line(j):
        def load():
            return cells[:, j].reshape(LINE, WIDTH).astype(jnp.float32)

        def store(done):
            for lanes in range(GROUPS):
                turned[lanes, pl.ds(j, LINE, stride=LINES), :] = done[:, lanes * HALF : (lanes + 1) * HALF]

        return Line(load, store, gain, qk_w, val_w, out_w, probs)

    attend([line(j) for j in range(LINES)])
    n_row, n_col, deep = out.shape[:3]
    for lanes in range(GROUPS):
        here = slice(lanes * HALF, (lanes + 1) * HALF)
        blocks = turned[lanes].astype(jnp.bfloat16).reshape(n_col, n_row, deep, HALF)
        for r in range(n_row):
            out[r, :, :, here] = blocks[:, r]


def col_kernel(cells, gain, qk_w, val_w, out_w, out, probs):

    def line(m):
        def load():
            tiles = cells[...].reshape(LINE // LINES, LINES * LINES, WIDTH)[:, m // 2 * 8 : m // 2 * 8 + 8]
            tiles = tiles.astype(jnp.float32).reshape(LINE // 8, 2, 8, WIDTH)
            even, odd = tiles[:, 0], tiles[:, 1]
            if m % 2:
                even = pltpu.roll(even, LINES, 1)
            else:
                odd = pltpu.roll(odd, LINES, 1)
            row = lax.broadcasted_iota(jnp.int32, even.shape, 1)
            return jnp.where(row < LINES, even, odd).reshape(LINE, WIDTH)

        def store(done):
            out[:, m] = done.astype(jnp.bfloat16).reshape(out.shape[0], out.shape[2], WIDTH)

        return Line(load, store, gain, qk_w, val_w, out_w, probs)

    attend([line(m) for m in range(LINES)])


def mlp_kernel(blocks, gain, in_w, out_w, out, swap, done, sems):
    rows, cols = out.shape[:2]
    deep = rows // LINES
    cells = deep * cols
    to = lax.broadcasted_iota(jnp.int32, (cells, cells), 0)
    come = lax.broadcasted_iota(jnp.int32, (cells, cells), 1)
    moved = come == to % cols * deep + to // cols
    swap[...] = jnp.where(moved, 1.0, 0.0).astype(jnp.bfloat16)
    parts = [slice(part * deep, (part + 1) * deep) for part in range(LINES)]
    lines = [matmul(swap[...], blocks[:, :, here].reshape(cells, WIDTH)) for here in parts]
    normed = [layer_norm(line, gain[...]).astype(jnp.bfloat16) for line in lines]
    copies = []
    for part, here in enumerate(parts):
        for start in range(0, cells, BLOCK):
            pre = matmul(normed[part][start : start + BLOCK], in_w[...])
            inner = jnp.tanh(pre * (GELU_A + GELU_B * (pre * pre)))
            hidden = (pre * (0.5 + 0.5 * inner)).astype(jnp.bfloat16)
            result = lines[part][start : start + BLOCK] + matmul(hidden, out_w[...])
            first = part * deep + start // cols
            done[first : first + BLOCK // cols] = result.astype(jnp.bfloat16).reshape(
                BLOCK // cols, cols, WIDTH
            )
        copies.append(pltpu.make_async_copy(done.at[here], out.at[here], sems.at[part]))
        copies[-1].start()
    for copy in copies:
        copy.wait()


IN_VMEM = pl.BlockSpec(memory_space=pltpu.VMEM)
PARAMS = pltpu.CompilerParams(vmem_limit_bytes=40 * 2**20)


def bf16(*shape):
    return jax.ShapeDtypeStruct(shape, jnp.bfloat16)


def attend_scratch():
    return [pltpu.VMEM((HEADS, LINE, LINE), jnp.bfloat16)]


def row_attention(n_row, strips, gain, qk_w, val_w, out_w, *gains):
    n_col = strips.shape[0]
    return pl.pallas_call(
        row_kernel,
        in_specs=[IN_VMEM] * 7,
        out_specs=[IN_VMEM] * 3,
        out_shape=[bf16(n_row, n_col, LINES * LINES, WIDTH)]
        + [jax.ShapeDtypeStruct(later.shape, later.dtype) for later in gains],
        scratch_shapes=attend_scratch() + [pltpu.VMEM((GROUPS, LINES * LINE, HALF), jnp.float32)],
        compiler_params=PARAMS,
        name="row_attention",
    )(strips, gain, qk_w, val_w, out_w, *gains)


def col_attention(n_row, columns, *weights):
    return pl.pallas_call(
        col_kernel,
        in_specs=[IN_VMEM] * 5,
        out_specs=IN_VMEM,
        out_shape=bf16(n_row, LINES, LINE // n_row, WIDTH),
        scratch_shapes=attend_scratch(),
        compiler_params=PARAMS,
        name="col_attention",
    )(columns, *weights)


def mlp(cols, blocks, *weights):
    rows = blocks.shape[2]
    cells = rows // LINES * cols
    return pl.pallas_call(
        mlp_kernel,
        in_specs=[IN_VMEM] * 4,
        out_specs=pl.BlockSpec(memory_space=pl.ANY),
        out_shape=bf16(rows, cols, WIDTH),
        scratch_shapes=[
            pltpu.VMEM((cells, cells), jnp.bfloat16),
            pltpu.VMEM((rows, cols, WIDTH), jnp.bfloat16),
            pltpu.SemaphoreType.DMA((LINES,)),
        ],
        compiler_params=PARAMS,
        name="mlp",
    )(blocks, *weights)


def per_device(
    cells,
    row_gain,
    row_qk,
    row_value,
    row_out,
    col_gain,
    col_qk,
    col_value,
    col_out,
    mlp_gain,
    mlp_in,
    mlp_out,
):
    n_row = lax.axis_size("row")
    n_col = lax.axis_size("col")
    rows, cols, width = cells.shape
    row_gain, col_gain, mlp_gain = (g.reshape(1, width) for g in (row_gain, col_gain, mlp_gain))
    strips = lax.all_to_all(cells, "col", split_axis=0, concat_axis=0, tiled=True)
    strips = strips.reshape(n_col, LINES, cols, width)
    after_rows, col_gain, mlp_gain = row_attention(
        n_row, strips, row_gain, row_qk, row_value, row_out, col_gain, mlp_gain
    )
    columns = lax.all_to_all(
        after_rows.reshape(-1, width), ("row", "col"), split_axis=0, concat_axis=0, tiled=True
    )
    after_cols = col_attention(n_row, columns, col_gain, col_qk, col_value, col_out)
    blocks = lax.all_to_all(
        after_cols.reshape(-1, width), "row", split_axis=0, concat_axis=0, tiled=True
    )
    return mlp(cols, blocks.reshape(n_row, LINES, rows, width), mlp_gain, mlp_in, mlp_out)


def solution(mesh):
    in_specs = (P("row", "col", None), P(), P(), P(), P(), P(), P(), P(), P(), P(), P(), P())
    out_specs = P("row", "col", None)
    return jax.shard_map(
        per_device, mesh=mesh, in_specs=in_specs, out_specs=out_specs, check_vma=False
    )
```

```python
import functools
import math

import jax
import jax.numpy as jnp
from jax import lax
from jax.experimental import pallas as pl
from jax.experimental.pallas import tpu as pltpu
from jax.sharding import PartitionSpec as P

HEADS = 8
HEAD = 32
WIDTH = 256
LINE = 512
LINES = 4
HALF = 128
GROUPS = 2
IN_GROUP = 4
BLOCK = 256
CHUNK = 256
LEAST, MOST = 2.0**-60, 2.0**100
SCALE = math.log2(math.e) / math.sqrt(HEAD)
GELU_A = math.sqrt(2.0 / math.pi)
GELU_B = GELU_A * 0.044715


def layer_norm(values, gain):
    mean = jnp.mean(values, axis=-1, keepdims=True)
    centred = values - mean
    variance = jnp.mean(centred * centred, axis=-1, keepdims=True)
    return centred * lax.rsqrt(variance + 1e-05) * gain


def matmul(left, right):
    return jnp.dot(left, right, preferred_element_type=jnp.float32)


def dot(left, right, left_dim, right_dim):
    return lax.dot_general(
        left, right, (((left_dim,), (right_dim,)), ((), ())), preferred_element_type=jnp.float32
    )


class Line:
    def __init__(self, shift, load, store, gain, qk_w, val_w, out_w, probs):
        self.shift = shift
        self.load, self.store = load, store
        self.gain, self.qk_w, self.val_w, self.out_w = gain, qk_w, val_w, out_w
        self.probs = probs
        self.chunk = CHUNK if shift else LINE
        self.largest = {}
        self.mixed = []
        self.fits = []

    def project(self):
        normed = layer_norm(self.load(), self.gain[...]).astype(jnp.bfloat16)
        both = matmul(normed, self.qk_w[...])
        self.values = dot(self.val_w[...], normed, 0, 1).astype(jnp.bfloat16)
        query = both[:, :WIDTH].astype(jnp.bfloat16).astype(jnp.float32) * SCALE
        self.query_hi = query.astype(jnp.bfloat16)
        self.query_lo = (query - self.query_hi.astype(jnp.float32)).astype(jnp.bfloat16)
        self.keys = both[:, WIDTH:].astype(jnp.bfloat16)

    def weigh(self, group):
        lanes = slice(group * HALF, (group + 1) * HALF)
        query = jnp.concatenate([self.query_hi[:, lanes], self.query_lo[:, lanes]], axis=1)
        keys = self.keys[:, lanes]
        zero = jnp.zeros_like(keys)
        lane = lax.broadcasted_iota(jnp.int32, (LINE, HALF), 1) // HEAD
        for head in range(IN_GROUP):
            head_keys = jnp.where(lane == head, keys, zero)
            head_keys = jnp.concatenate([head_keys, head_keys], axis=1)
            for start in range(0, LINE, BLOCK):
                here = slice(start, start + BLOCK)
                for chunk in range(0, LINE, self.chunk):
                    rows = slice(chunk, chunk + self.chunk)
                    scores = dot(head_keys[rows], query[here], 1, 1)
                    if self.shift:
                        largest = jnp.max(scores, axis=0, keepdims=True)
                        self.largest[group, head, chunk, start] = largest
                        scores = scores - largest
                    weights = jnp.exp2(scores).astype(jnp.bfloat16)
                    self.probs[group * IN_GROUP + head, rows, here] = weights

    def mix(self, group):
        ones = jnp.ones((16, LINE), jnp.bfloat16)
        for head in range(IN_GROUP):
            index = group * IN_GROUP + head
            values = jnp.concatenate([self.values[index * HEAD : (index + 1) * HEAD], ones], axis=0)
            if self.shift:
                total = self.sum_chunks(group, head, values)
            else:
                total = matmul(values, self.probs[index])
                weight = total[HEAD : HEAD + 1]
                fits = (weight >= LEAST) & (weight <= MOST)
                self.fits.append(jnp.where(fits, 1.0, 0.0))
            self.mixed.append((total[:HEAD] / total[HEAD : HEAD + 1]).astype(jnp.bfloat16))

    def sum_chunks(self, group, head, values):
        chunks = range(0, LINE, self.chunk)
        scales = [
            jnp.concatenate(
                [self.largest[group, head, chunk, start] for start in range(0, LINE, BLOCK)], axis=1
            )
            for chunk in chunks
        ]
        largest = functools.reduce(jnp.maximum, scales)
        total = 0.0
        for chunk, scale in zip(chunks, scales):
            rows = slice(chunk, chunk + self.chunk)
            part = matmul(values[:, rows], self.probs[group * IN_GROUP + head, rows])
            total += part * jnp.exp2(scale - largest)
        return total

    def finish(self):
        self.store(self.load() + dot(jnp.concatenate(self.mixed, axis=0), self.out_w[...], 0, 0))


def run(lines):
    lines[0].project()
    lines[0].weigh(0)
    for line, later in zip(lines, lines[1:] + [None]):
        line.mix(0)
        line.weigh(1)
        if later is not None:
            later.project()
        line.mix(1)
        if later is not None:
            later.weigh(0)
        line.finish()


def attend(make):
    lines = [make(False, j) for j in range(LINES)]
    run(lines)
    fits = functools.reduce(jnp.minimum, [part for line in lines for part in line.fits])

    @pl.when(jnp.min(fits) < 0.5)
    def _():
        run([make(True, j) for j in range(LINES)])


def row_kernel(
    cells, gain, qk_w, val_w, out_w, later_gain, last_gain, out, later_out, last_out, probs, turned
):
    later_out[...] = later_gain[...]
    last_out[...] = last_gain[...]

    def line(shift, j):
        def load():
            return cells[:, j].reshape(LINE, WIDTH).astype(jnp.float32)

        def store(done):
            for lanes in range(GROUPS):
                turned[lanes, pl.ds(j, LINE, stride=LINES), :] = done[:, lanes * HALF : (lanes + 1) * HALF]

        return Line(shift, load, store, gain, qk_w, val_w, out_w, probs)

    attend(line)
    n_row, n_col, deep = out.shape[:3]
    for lanes in range(GROUPS):
        here = slice(lanes * HALF, (lanes + 1) * HALF)
        blocks = turned[lanes].astype(jnp.bfloat16).reshape(n_col, n_row, deep, HALF)
        for r in range(n_row):
            out[r, :, :, here] = blocks[:, r]


def col_kernel(cells, gain, qk_w, val_w, out_w, out, probs):

    def line(shift, m):
        def load():
            tiles = cells[...].reshape(LINE // LINES, LINES * LINES, WIDTH)[:, m // 2 * 8 : m // 2 * 8 + 8]
            tiles = tiles.astype(jnp.float32).reshape(LINE // 8, 2, 8, WIDTH)
            even, odd = tiles[:, 0], tiles[:, 1]
            if m % 2:
                even = pltpu.roll(even, LINES, 1)
            else:
                odd = pltpu.roll(odd, LINES, 1)
            row = lax.broadcasted_iota(jnp.int32, even.shape, 1)
            return jnp.where(row < LINES, even, odd).reshape(LINE, WIDTH)

        def store(done):
            out[:, m] = done.astype(jnp.bfloat16).reshape(out.shape[0], out.shape[2], WIDTH)

        return Line(shift, load, store, gain, qk_w, val_w, out_w, probs)

    attend(line)


def mlp_kernel(blocks, gain, in_w, out_w, out, swap, done, sems):
    rows, cols = out.shape[:2]
    deep = rows // LINES
    cells = deep * cols
    to = lax.broadcasted_iota(jnp.int32, (cells, cells), 0)
    come = lax.broadcasted_iota(jnp.int32, (cells, cells), 1)
    moved = come == to % cols * deep + to // cols
    swap[...] = jnp.where(moved, 1.0, 0.0).astype(jnp.bfloat16)
    parts = [slice(part * deep, (part + 1) * deep) for part in range(LINES)]
    lines = [matmul(swap[...], blocks[:, :, here].reshape(cells, WIDTH)) for here in parts]
    normed = [layer_norm(line, gain[...]).astype(jnp.bfloat16) for line in lines]
    copies = []
    for part, here in enumerate(parts):
        for start in range(0, cells, BLOCK):
            pre = matmul(normed[part][start : start + BLOCK], in_w[...])
            inner = jnp.tanh(pre * (GELU_A + GELU_B * (pre * pre)))
            hidden = (pre * (0.5 + 0.5 * inner)).astype(jnp.bfloat16)
            result = lines[part][start : start + BLOCK] + matmul(hidden, out_w[...])
            first = part * deep + start // cols
            done[first : first + BLOCK // cols] = result.astype(jnp.bfloat16).reshape(
                BLOCK // cols, cols, WIDTH
            )
        copies.append(pltpu.make_async_copy(done.at[here], out.at[here], sems.at[part]))
        copies[-1].start()
    for copy in copies:
        copy.wait()


IN_VMEM = pl.BlockSpec(memory_space=pltpu.VMEM)
PARAMS = pltpu.CompilerParams(vmem_limit_bytes=40 * 2**20)


def bf16(*shape):
    return jax.ShapeDtypeStruct(shape, jnp.bfloat16)


def attend_scratch():
    return [pltpu.VMEM((HEADS, LINE, LINE), jnp.bfloat16)]


def row_attention(n_row, strips, gain, qk_w, val_w, out_w, *gains):
    n_col = strips.shape[0]
    return pl.pallas_call(
        row_kernel,
        in_specs=[IN_VMEM] * 7,
        out_specs=[IN_VMEM] * 3,
        out_shape=[bf16(n_row, n_col, LINES * LINES, WIDTH)]
        + [jax.ShapeDtypeStruct(later.shape, later.dtype) for later in gains],
        scratch_shapes=attend_scratch() + [pltpu.VMEM((GROUPS, LINES * LINE, HALF), jnp.float32)],
        compiler_params=PARAMS,
        name="row_attention",
    )(strips, gain, qk_w, val_w, out_w, *gains)


def col_attention(n_row, columns, *weights):
    return pl.pallas_call(
        col_kernel,
        in_specs=[IN_VMEM] * 5,
        out_specs=IN_VMEM,
        out_shape=bf16(n_row, LINES, LINE // n_row, WIDTH),
        scratch_shapes=attend_scratch(),
        compiler_params=PARAMS,
        name="col_attention",
    )(columns, *weights)


def mlp(cols, blocks, *weights):
    rows = blocks.shape[2]
    cells = rows // LINES * cols
    return pl.pallas_call(
        mlp_kernel,
        in_specs=[IN_VMEM] * 4,
        out_specs=pl.BlockSpec(memory_space=pl.ANY),
        out_shape=bf16(rows, cols, WIDTH),
        scratch_shapes=[
            pltpu.VMEM((cells, cells), jnp.bfloat16),
            pltpu.VMEM((rows, cols, WIDTH), jnp.bfloat16),
            pltpu.SemaphoreType.DMA((LINES,)),
        ],
        compiler_params=PARAMS,
        name="mlp",
    )(blocks, *weights)


def per_device(
    cells,
    row_gain,
    row_qk,
    row_value,
    row_out,
    col_gain,
    col_qk,
    col_value,
    col_out,
    mlp_gain,
    mlp_in,
    mlp_out,
):
    n_row = lax.axis_size("row")
    n_col = lax.axis_size("col")
    rows, cols, width = cells.shape
    row_gain, col_gain, mlp_gain = (g.reshape(1, width) for g in (row_gain, col_gain, mlp_gain))
    strips = lax.all_to_all(cells, "col", split_axis=0, concat_axis=0, tiled=True)
    strips = strips.reshape(n_col, LINES, cols, width)
    after_rows, col_gain, mlp_gain = row_attention(
        n_row, strips, row_gain, row_qk, row_value, row_out, col_gain, mlp_gain
    )
    columns = lax.all_to_all(
        after_rows.reshape(-1, width), ("row", "col"), split_axis=0, concat_axis=0, tiled=True
    )
    after_cols = col_attention(n_row, columns, col_gain, col_qk, col_value, col_out)
    blocks = lax.all_to_all(
        after_cols.reshape(-1, width), "row", split_axis=0, concat_axis=0, tiled=True
    )
    return mlp(cols, blocks.reshape(n_row, LINES, rows, width), mlp_gain, mlp_in, mlp_out)


def solution(mesh):
    in_specs = (P("row", "col", None), P(), P(), P(), P(), P(), P(), P(), P(), P(), P(), P())
    out_specs = P("row", "col", None)
    return jax.shard_map(
        per_device, mesh=mesh, in_specs=in_specs, out_specs=out_specs, check_vma=False
    )
```

```python
import functools
import math

import jax
import jax.numpy as jnp
from jax import lax
from jax.experimental import pallas as pl
from jax.experimental.pallas import tpu as pltpu
from jax.sharding import PartitionSpec as P

HEADS = 8
HEAD = 32
WIDTH = 256
LINE = 512
LINES = 4
HALF = 128
GROUPS = 2
IN_GROUP = 4
BLOCK = 256
CHUNK = 256
LEAST, MOST = 2.0**-60, 2.0**100
SCALE = math.log2(math.e) / math.sqrt(HEAD)
GELU_A = math.sqrt(2.0 / math.pi)
GELU_B = GELU_A * 0.044715


def layer_norm(values, gain):
    mean = jnp.mean(values, axis=-1, keepdims=True)
    centred = values - mean
    variance = jnp.mean(centred * centred, axis=-1, keepdims=True)
    return centred * lax.rsqrt(variance + 1e-05) * gain


def matmul(left, right):
    return jnp.dot(left, right, preferred_element_type=jnp.float32)


def dot(left, right, left_dim, right_dim):
    return lax.dot_general(
        left, right, (((left_dim,), (right_dim,)), ((), ())), preferred_element_type=jnp.float32
    )


class Line:
    def __init__(self, shift, load, store, gain, qk_w, val_w, out_w, probs):
        self.shift = shift
        self.load, self.store = load, store
        self.gain, self.qk_w, self.val_w, self.out_w = gain, qk_w, val_w, out_w
        self.probs = probs
        self.chunk = CHUNK if shift else LINE
        self.largest = {}
        self.mixed = []
        self.fits = []

    def project(self):
        normed = layer_norm(self.load(), self.gain[...]).astype(jnp.bfloat16)
        both = matmul(normed, self.qk_w[...])
        self.values = dot(self.val_w[...], normed, 0, 1).astype(jnp.bfloat16)
        query = both[:, :WIDTH].astype(jnp.bfloat16).astype(jnp.float32) * SCALE
        self.query_hi = query.astype(jnp.bfloat16)
        self.query_lo = (query - self.query_hi.astype(jnp.float32)).astype(jnp.bfloat16)
        self.keys = both[:, WIDTH:].astype(jnp.bfloat16)

    def weigh(self, group):
        lanes = slice(group * HALF, (group + 1) * HALF)
        query = jnp.concatenate([self.query_hi[:, lanes], self.query_lo[:, lanes]], axis=1)
        keys = self.keys[:, lanes]
        zero = jnp.zeros_like(keys)
        lane = lax.broadcasted_iota(jnp.int32, (LINE, HALF), 1) // HEAD
        for head in range(IN_GROUP):
            head_keys = jnp.where(lane == head, keys, zero)
            head_keys = jnp.concatenate([head_keys, head_keys], axis=1)
            for start in range(0, LINE, BLOCK):
                here = slice(start, start + BLOCK)
                for chunk in range(0, LINE, self.chunk):
                    rows = slice(chunk, chunk + self.chunk)
                    scores = dot(head_keys[rows], query[here], 1, 1)
                    if self.shift:
                        largest = jnp.max(scores, axis=0, keepdims=True)
                        self.largest[group, head, chunk, start] = largest
                        scores = scores - largest
                    weights = jnp.exp2(scores).astype(jnp.bfloat16)
                    self.probs[group * IN_GROUP + head, rows, here] = weights

    def mix(self, group):
        ones = jnp.ones((16, LINE), jnp.bfloat16)
        for head in range(IN_GROUP):
            index = group * IN_GROUP + head
            values = jnp.concatenate([self.values[index * HEAD : (index + 1) * HEAD], ones], axis=0)
            if self.shift:
                total = self.sum_chunks(group, head, values)
            else:
                total = matmul(values, self.probs[index])
                weight = total[HEAD : HEAD + 1]
                fits = (weight >= LEAST) & (weight <= MOST)
                self.fits.append(jnp.where(fits, 1.0, 0.0))
            self.mixed.append((total[:HEAD] / total[HEAD : HEAD + 1]).astype(jnp.bfloat16))

    def sum_chunks(self, group, head, values):
        chunks = range(0, LINE, self.chunk)
        scales = [
            jnp.concatenate(
                [self.largest[group, head, chunk, start] for start in range(0, LINE, BLOCK)], axis=1
            )
            for chunk in chunks
        ]
        largest = functools.reduce(jnp.maximum, scales)
        total = 0.0
        for chunk, scale in zip(chunks, scales):
            rows = slice(chunk, chunk + self.chunk)
            part = matmul(values[:, rows], self.probs[group * IN_GROUP + head, rows])
            total += part * jnp.exp2(scale - largest)
        return total

    def finish(self):
        self.store(self.load() + dot(jnp.concatenate(self.mixed, axis=0), self.out_w[...], 0, 0))


def run(lines):
    lines[0].project()
    lines[0].weigh(0)
    for line, later in zip(lines, lines[1:] + [None]):
        line.mix(0)
        line.weigh(1)
        if later is not None:
            later.project()
        line.mix(1)
        if later is not None:
            later.weigh(0)
        line.finish()


def attend(make):
    lines = [make(False, j) for j in range(LINES)]
    run(lines)
    fits = functools.reduce(jnp.minimum, [part for line in lines for part in line.fits])

    @pl.when(jnp.min(fits) < 0.5)
    def _():
        def again(j, carry):
            run([make(True, j)])
            return carry

        lax.fori_loop(0, LINES, again, 0)


def pick(first, left, right):
    if isinstance(first, bool):
        return left if first else right
    return jnp.where(first, left, right)


def row_kernel(
    cells, gain, qk_w, val_w, out_w, later_gain, last_gain, out, later_out, last_out, probs, turned
):
    later_out[...] = later_gain[...]
    last_out[...] = last_gain[...]

    def line(shift, j):
        def load():
            return cells[:, j].reshape(LINE, WIDTH).astype(jnp.float32)

        def store(done):
            for lanes in range(GROUPS):
                turned[lanes, pl.ds(j, LINE, stride=LINES), :] = done[:, lanes * HALF : (lanes + 1) * HALF]

        return Line(shift, load, store, gain, qk_w, val_w, out_w, probs)

    attend(line)
    n_row, n_col, deep = out.shape[:3]
    for lanes in range(GROUPS):
        here = slice(lanes * HALF, (lanes + 1) * HALF)
        blocks = turned[lanes].astype(jnp.bfloat16).reshape(n_col, n_row, deep, HALF)
        for r in range(n_row):
            out[r, :, :, here] = blocks[:, r]


def col_kernel(cells, gain, qk_w, val_w, out_w, out, probs):

    def line(shift, m):
        def load():
            tiles = cells[...].reshape(LINE // LINES, LINES * LINES, WIDTH)
            tiles = pick(m < 2, tiles[:, :8], tiles[:, 8:])
            tiles = tiles.astype(jnp.float32).reshape(LINE // 8, 2, 8, WIDTH)
            even, odd = tiles[:, 0], tiles[:, 1]
            first = m % 2 == 0
            even = pick(first, even, pltpu.roll(even, LINES, 1))
            odd = pick(first, pltpu.roll(odd, LINES, 1), odd)
            row = lax.broadcasted_iota(jnp.int32, even.shape, 1)
            return jnp.where(row < LINES, even, odd).reshape(LINE, WIDTH)

        def store(done):
            out[:, m] = done.astype(jnp.bfloat16).reshape(out.shape[0], out.shape[2], WIDTH)

        return Line(shift, load, store, gain, qk_w, val_w, out_w, probs)

    attend(line)


def mlp_kernel(blocks, gain, in_w, out_w, out, swap, done, sems):
    rows, cols = out.shape[:2]
    deep = rows // LINES
    cells = deep * cols
    to = lax.broadcasted_iota(jnp.int32, (cells, cells), 0)
    come = lax.broadcasted_iota(jnp.int32, (cells, cells), 1)
    moved = come == to % cols * deep + to // cols
    swap[...] = jnp.where(moved, 1.0, 0.0).astype(jnp.bfloat16)
    parts = [slice(part * deep, (part + 1) * deep) for part in range(LINES)]
    lines = [matmul(swap[...], blocks[:, :, here].reshape(cells, WIDTH)) for here in parts]
    normed = [layer_norm(line, gain[...]).astype(jnp.bfloat16) for line in lines]
    copies = []
    for part, here in enumerate(parts):
        for start in range(0, cells, BLOCK):
            pre = matmul(normed[part][start : start + BLOCK], in_w[...])
            inner = jnp.tanh(pre * (GELU_A + GELU_B * (pre * pre)))
            hidden = (pre * (0.5 + 0.5 * inner)).astype(jnp.bfloat16)
            result = lines[part][start : start + BLOCK] + matmul(hidden, out_w[...])
            first = part * deep + start // cols
            done[first : first + BLOCK // cols] = result.astype(jnp.bfloat16).reshape(
                BLOCK // cols, cols, WIDTH
            )
        copies.append(pltpu.make_async_copy(done.at[here], out.at[here], sems.at[part]))
        copies[-1].start()
    for copy in copies:
        copy.wait()


IN_VMEM = pl.BlockSpec(memory_space=pltpu.VMEM)
PARAMS = pltpu.CompilerParams(vmem_limit_bytes=40 * 2**20)


def bf16(*shape):
    return jax.ShapeDtypeStruct(shape, jnp.bfloat16)


def attend_scratch():
    return [pltpu.VMEM((HEADS, LINE, LINE), jnp.bfloat16)]


def row_attention(n_row, strips, gain, qk_w, val_w, out_w, *gains):
    n_col = strips.shape[0]
    return pl.pallas_call(
        row_kernel,
        in_specs=[IN_VMEM] * 7,
        out_specs=[IN_VMEM] * 3,
        out_shape=[bf16(n_row, n_col, LINES * LINES, WIDTH)]
        + [jax.ShapeDtypeStruct(later.shape, later.dtype) for later in gains],
        scratch_shapes=attend_scratch() + [pltpu.VMEM((GROUPS, LINES * LINE, HALF), jnp.float32)],
        compiler_params=PARAMS,
        name="row_attention",
    )(strips, gain, qk_w, val_w, out_w, *gains)


def col_attention(n_row, columns, *weights):
    return pl.pallas_call(
        col_kernel,
        in_specs=[IN_VMEM] * 5,
        out_specs=IN_VMEM,
        out_shape=bf16(n_row, LINES, LINE // n_row, WIDTH),
        scratch_shapes=attend_scratch(),
        compiler_params=PARAMS,
        name="col_attention",
    )(columns, *weights)


def mlp(cols, blocks, *weights):
    rows = blocks.shape[2]
    cells = rows // LINES * cols
    return pl.pallas_call(
        mlp_kernel,
        in_specs=[IN_VMEM] * 4,
        out_specs=pl.BlockSpec(memory_space=pl.ANY),
        out_shape=bf16(rows, cols, WIDTH),
        scratch_shapes=[
            pltpu.VMEM((cells, cells), jnp.bfloat16),
            pltpu.VMEM((rows, cols, WIDTH), jnp.bfloat16),
            pltpu.SemaphoreType.DMA((LINES,)),
        ],
        compiler_params=PARAMS,
        name="mlp",
    )(blocks, *weights)


def per_device(
    cells,
    row_gain,
    row_qk,
    row_value,
    row_out,
    col_gain,
    col_qk,
    col_value,
    col_out,
    mlp_gain,
    mlp_in,
    mlp_out,
):
    n_row = lax.axis_size("row")
    n_col = lax.axis_size("col")
    rows, cols, width = cells.shape
    row_gain, col_gain, mlp_gain = (g.reshape(1, width) for g in (row_gain, col_gain, mlp_gain))
    strips = lax.all_to_all(cells, "col", split_axis=0, concat_axis=0, tiled=True)
    strips = strips.reshape(n_col, LINES, cols, width)
    after_rows, col_gain, mlp_gain = row_attention(
        n_row, strips, row_gain, row_qk, row_value, row_out, col_gain, mlp_gain
    )
    columns = lax.all_to_all(
        after_rows.reshape(-1, width), ("row", "col"), split_axis=0, concat_axis=0, tiled=True
    )
    after_cols = col_attention(n_row, columns, col_gain, col_qk, col_value, col_out)
    blocks = lax.all_to_all(
        after_cols.reshape(-1, width), "row", split_axis=0, concat_axis=0, tiled=True
    )
    return mlp(cols, blocks.reshape(n_row, LINES, rows, width), mlp_gain, mlp_in, mlp_out)


def solution(mesh):
    in_specs = (P("row", "col", None), P(), P(), P(), P(), P(), P(), P(), P(), P(), P(), P())
    out_specs = P("row", "col", None)
    return jax.shard_map(
        per_device, mesh=mesh, in_specs=in_specs, out_specs=out_specs, check_vma=False
    )
```

```python
import functools
import math

import jax
import jax.numpy as jnp
from jax import lax
from jax.experimental import pallas as pl
from jax.experimental.pallas import tpu as pltpu
from jax.sharding import PartitionSpec as P

HEADS = 8
HEAD = 32
WIDTH = 256
LINE = 512
LINES = 4
HALF = 128
GROUPS = 2
IN_GROUP = 4
BLOCK = 256
CHUNK = 256
LEAST, MOST = 2.0**-60, 2.0**100
SCALE = math.log2(math.e) / math.sqrt(HEAD)
GELU_A = math.sqrt(2.0 / math.pi)
GELU_B = GELU_A * 0.044715


def layer_norm(values, gain):
    mean = jnp.mean(values, axis=-1, keepdims=True)
    centred = values - mean
    variance = jnp.mean(centred * centred, axis=-1, keepdims=True)
    return centred * lax.rsqrt(variance + 1e-05) * gain


def matmul(left, right):
    return jnp.dot(left, right, preferred_element_type=jnp.float32)


def dot(left, right, left_dim, right_dim):
    return lax.dot_general(
        left, right, (((left_dim,), (right_dim,)), ((), ())), preferred_element_type=jnp.float32
    )


class Line:
    def __init__(self, shift, load, store, gain, qk_w, val_w, out_w, probs):
        self.shift = shift
        self.load, self.store = load, store
        self.gain, self.qk_w, self.val_w, self.out_w = gain, qk_w, val_w, out_w
        self.probs = probs
        self.chunk = CHUNK if shift else LINE
        self.largest = {}
        self.mixed = []
        self.fits = []

    def project(self):
        normed = layer_norm(self.load(), self.gain[...]).astype(jnp.bfloat16)
        both = matmul(normed, self.qk_w[...])
        self.values = dot(self.val_w[...], normed, 0, 1).astype(jnp.bfloat16)
        query = both[:, :WIDTH].astype(jnp.bfloat16).astype(jnp.float32) * SCALE
        self.query_hi = query.astype(jnp.bfloat16)
        self.query_lo = (query - self.query_hi.astype(jnp.float32)).astype(jnp.bfloat16)
        self.keys = both[:, WIDTH:].astype(jnp.bfloat16)

    def weigh(self, group):
        lanes = slice(group * HALF, (group + 1) * HALF)
        query = jnp.concatenate([self.query_hi[:, lanes], self.query_lo[:, lanes]], axis=1)
        keys = self.keys[:, lanes]
        zero = jnp.zeros_like(keys)
        lane = lax.broadcasted_iota(jnp.int32, (LINE, HALF), 1) // HEAD
        for head in range(IN_GROUP):
            head_keys = jnp.where(lane == head, keys, zero)
            head_keys = jnp.concatenate([head_keys, head_keys], axis=1)
            for start in range(0, LINE, BLOCK):
                here = slice(start, start + BLOCK)
                for chunk in range(0, LINE, self.chunk):
                    rows = slice(chunk, chunk + self.chunk)
                    scores = dot(head_keys[rows], query[here], 1, 1)
                    if self.shift:
                        largest = jnp.max(scores, axis=0, keepdims=True)
                        self.largest[group, head, chunk, start] = largest
                        scores = scores - largest
                    weights = jnp.exp2(scores).astype(jnp.bfloat16)
                    self.probs[group * IN_GROUP + head, rows, here] = weights

    def mix(self, group):
        ones = jnp.ones((16, LINE), jnp.bfloat16)
        for head in range(IN_GROUP):
            index = group * IN_GROUP + head
            values = jnp.concatenate([self.values[index * HEAD : (index + 1) * HEAD], ones], axis=0)
            if self.shift:
                total = self.sum_chunks(group, head, values)
            else:
                total = matmul(values, self.probs[index])
                weight = total[HEAD : HEAD + 1]
                fits = (weight >= LEAST) & (weight <= MOST)
                self.fits.append(jnp.where(fits, 1.0, 0.0))
            self.mixed.append((total[:HEAD] * (1.0 / total[HEAD : HEAD + 1])).astype(jnp.bfloat16))

    def sum_chunks(self, group, head, values):
        chunks = range(0, LINE, self.chunk)
        scales = [
            jnp.concatenate(
                [self.largest[group, head, chunk, start] for start in range(0, LINE, BLOCK)], axis=1
            )
            for chunk in chunks
        ]
        largest = functools.reduce(jnp.maximum, scales)
        total = 0.0
        for chunk, scale in zip(chunks, scales):
            rows = slice(chunk, chunk + self.chunk)
            part = matmul(values[:, rows], self.probs[group * IN_GROUP + head, rows])
            total += part * jnp.exp2(scale - largest)
        return total

    def finish(self):
        self.store(self.load() + dot(jnp.concatenate(self.mixed, axis=0), self.out_w[...], 0, 0))


def run(lines):
    lines[0].project()
    lines[0].weigh(0)
    for line, later in zip(lines, lines[1:] + [None]):
        line.mix(0)
        line.weigh(1)
        if later is not None:
            later.project()
        line.mix(1)
        if later is not None:
            later.weigh(0)
        line.finish()


def attend(make):
    lines = [make(False, j) for j in range(LINES)]
    run(lines)
    fits = functools.reduce(jnp.minimum, [part for line in lines for part in line.fits])

    @pl.when(jnp.min(fits) < 0.5)
    def _():
        def again(j, carry):
            run([make(True, j)])
            return carry

        lax.fori_loop(0, LINES, again, 0)


def pick(first, left, right):
    if isinstance(first, bool):
        return left if first else right
    return jnp.where(first, left, right)


def row_kernel(
    cells, gain, qk_w, val_w, out_w, later_gain, last_gain, out, later_out, last_out, probs, turned
):
    later_out[...] = later_gain[...]
    last_out[...] = last_gain[...]

    def line(shift, j):
        def load():
            return cells[:, j].reshape(LINE, WIDTH).astype(jnp.float32)

        def store(done):
            for lanes in range(GROUPS):
                turned[lanes, pl.ds(j, LINE, stride=LINES), :] = done[:, lanes * HALF : (lanes + 1) * HALF]

        return Line(shift, load, store, gain, qk_w, val_w, out_w, probs)

    attend(line)
    n_row, n_col, deep = out.shape[:3]
    for lanes in range(GROUPS):
        here = slice(lanes * HALF, (lanes + 1) * HALF)
        blocks = turned[lanes].astype(jnp.bfloat16).reshape(n_col, n_row, deep, HALF)
        for r in range(n_row):
            out[r, :, :, here] = blocks[:, r]


def col_kernel(cells, gain, qk_w, val_w, out_w, out, probs):

    def line(shift, m):
        def load():
            tiles = cells[...].reshape(LINE // LINES, LINES * LINES, WIDTH).astype(jnp.float32)
            tiles = pick(m < 2, tiles[:, :8], tiles[:, 8:]).reshape(LINE // 8, 2, 8, WIDTH)
            even, odd = tiles[:, 0], tiles[:, 1]
            first = m % 2 == 0
            even = pick(first, even, pltpu.roll(even, LINES, 1))
            odd = pick(first, pltpu.roll(odd, LINES, 1), odd)
            row = lax.broadcasted_iota(jnp.int32, even.shape, 1)
            return jnp.where(row < LINES, even, odd).reshape(LINE, WIDTH)

        def store(done):
            out[:, m] = done.astype(jnp.bfloat16).reshape(out.shape[0], out.shape[2], WIDTH)

        return Line(shift, load, store, gain, qk_w, val_w, out_w, probs)

    attend(line)


def mlp_kernel(blocks, gain, in_w, out_w, out, swap, done, sems):
    rows, cols = out.shape[:2]
    deep = rows // LINES
    cells = deep * cols
    to = lax.broadcasted_iota(jnp.int32, (cells, cells), 0)
    come = lax.broadcasted_iota(jnp.int32, (cells, cells), 1)
    moved = come == to % cols * deep + to // cols
    swap[...] = jnp.where(moved, 1.0, 0.0).astype(jnp.bfloat16)
    parts = [slice(part * deep, (part + 1) * deep) for part in range(LINES)]
    lines = [matmul(swap[...], blocks[:, :, here].reshape(cells, WIDTH)) for here in parts]
    normed = [layer_norm(line, gain[...]).astype(jnp.bfloat16) for line in lines]
    copies = []

    def widen(part):
        pre = matmul(normed[part], in_w[...])
        inner = jnp.tanh(pre * (GELU_A + GELU_B * (pre * pre)))
        return (pre * (0.5 + 0.5 * inner)).astype(jnp.bfloat16)

    hidden = widen(0)
    for part, here in enumerate(parts):
        later = widen(part + 1) if part + 1 < LINES else None
        result = lines[part] + matmul(hidden, out_w[...])
        done[here] = result.astype(jnp.bfloat16).reshape(deep, cols, WIDTH)
        copies.append(pltpu.make_async_copy(done.at[here], out.at[here], sems.at[part]))
        copies[-1].start()
        hidden = later
    for copy in copies:
        copy.wait()


IN_VMEM = pl.BlockSpec(memory_space=pltpu.VMEM)
PARAMS = pltpu.CompilerParams(vmem_limit_bytes=40 * 2**20)


def bf16(*shape):
    return jax.ShapeDtypeStruct(shape, jnp.bfloat16)


def attend_scratch():
    return [pltpu.VMEM((HEADS, LINE, LINE), jnp.bfloat16)]


def row_attention(n_row, strips, gain, qk_w, val_w, out_w, *gains):
    n_col = strips.shape[0]
    return pl.pallas_call(
        row_kernel,
        in_specs=[IN_VMEM] * 7,
        out_specs=[IN_VMEM] * 3,
        out_shape=[bf16(n_row, n_col, LINES * LINES, WIDTH)]
        + [jax.ShapeDtypeStruct(later.shape, later.dtype) for later in gains],
        scratch_shapes=attend_scratch() + [pltpu.VMEM((GROUPS, LINES * LINE, HALF), jnp.float32)],
        compiler_params=PARAMS,
        name="row_attention",
    )(strips, gain, qk_w, val_w, out_w, *gains)


def col_attention(n_row, columns, *weights):
    return pl.pallas_call(
        col_kernel,
        in_specs=[IN_VMEM] * 5,
        out_specs=IN_VMEM,
        out_shape=bf16(n_row, LINES, LINE // n_row, WIDTH),
        scratch_shapes=attend_scratch(),
        compiler_params=PARAMS,
        name="col_attention",
    )(columns, *weights)


def mlp(cols, blocks, *weights):
    rows = blocks.shape[2]
    cells = rows // LINES * cols
    return pl.pallas_call(
        mlp_kernel,
        in_specs=[IN_VMEM] * 4,
        out_specs=pl.BlockSpec(memory_space=pl.ANY),
        out_shape=bf16(rows, cols, WIDTH),
        scratch_shapes=[
            pltpu.VMEM((cells, cells), jnp.bfloat16),
            pltpu.VMEM((rows, cols, WIDTH), jnp.bfloat16),
            pltpu.SemaphoreType.DMA((LINES,)),
        ],
        compiler_params=PARAMS,
        name="mlp",
    )(blocks, *weights)


def per_device(
    cells,
    row_gain,
    row_qk,
    row_value,
    row_out,
    col_gain,
    col_qk,
    col_value,
    col_out,
    mlp_gain,
    mlp_in,
    mlp_out,
):
    n_row = lax.axis_size("row")
    n_col = lax.axis_size("col")
    rows, cols, width = cells.shape
    row_gain, col_gain, mlp_gain = (g.reshape(1, width) for g in (row_gain, col_gain, mlp_gain))
    strips = lax.all_to_all(cells, "col", split_axis=0, concat_axis=0, tiled=True)
    strips = strips.reshape(n_col, LINES, cols, width)
    after_rows, col_gain, mlp_gain = row_attention(
        n_row, strips, row_gain, row_qk, row_value, row_out, col_gain, mlp_gain
    )
    columns = lax.all_to_all(
        after_rows.reshape(-1, width), ("row", "col"), split_axis=0, concat_axis=0, tiled=True
    )
    after_cols = col_attention(n_row, columns, col_gain, col_qk, col_value, col_out)
    blocks = lax.all_to_all(
        after_cols.reshape(-1, width), "row", split_axis=0, concat_axis=0, tiled=True
    )
    return mlp(cols, blocks.reshape(n_row, LINES, rows, width), mlp_gain, mlp_in, mlp_out)


def solution(mesh):
    in_specs = (P("row", "col", None), P(), P(), P(), P(), P(), P(), P(), P(), P(), P(), P())
    out_specs = P("row", "col", None)
    return jax.shard_map(
        per_device, mesh=mesh, in_specs=in_specs, out_specs=out_specs, check_vma=False
    )
```

```python
import functools
import math

import jax
import jax.numpy as jnp
from jax import lax
from jax.experimental import pallas as pl
from jax.experimental.pallas import tpu as pltpu
from jax.sharding import PartitionSpec as P

HEADS = 8
HEAD = 32
WIDTH = 256
LINE = 512
LINES = 4
HALF = 128
GROUPS = 2
IN_GROUP = 4
BLOCK = 256
CHUNK = 256
LEAST, MOST = 2.0**-60, 2.0**100
SCALE = math.log2(math.e) / math.sqrt(HEAD)
GELU_A = math.sqrt(2.0 / math.pi)
GELU_B = GELU_A * 0.044715


def layer_norm(values, gain):
    mean = jnp.mean(values, axis=-1, keepdims=True)
    centred = values - mean
    variance = jnp.mean(centred * centred, axis=-1, keepdims=True)
    return centred * lax.rsqrt(variance + 1e-05) * gain


def matmul(left, right):
    return jnp.dot(left, right, preferred_element_type=jnp.float32)


def dot(left, right, left_dim, right_dim):
    return lax.dot_general(
        left, right, (((left_dim,), (right_dim,)), ((), ())), preferred_element_type=jnp.float32
    )


class Line:
    def __init__(self, shift, load, store, gain, qk_w, val_w, out_w, probs):
        self.shift = shift
        self.load, self.store = load, store
        self.gain, self.qk_w, self.val_w, self.out_w = gain, qk_w, val_w, out_w
        self.probs = probs
        self.chunk = CHUNK if shift else LINE
        self.largest = {}
        self.mixed = []
        self.fits = []

    def project(self):
        normed = layer_norm(self.load(), self.gain[...]).astype(jnp.bfloat16)
        both = matmul(normed, self.qk_w[...])
        self.values = dot(self.val_w[...], normed, 0, 1).astype(jnp.bfloat16)
        query = both[:, :WIDTH].astype(jnp.bfloat16).astype(jnp.float32) * SCALE
        self.query_hi = query.astype(jnp.bfloat16)
        self.query_lo = (query - self.query_hi.astype(jnp.float32)).astype(jnp.bfloat16)
        self.keys = both[:, WIDTH:].astype(jnp.bfloat16)

    def weigh(self, group):
        lanes = slice(group * HALF, (group + 1) * HALF)
        query = jnp.concatenate([self.query_hi[:, lanes], self.query_lo[:, lanes]], axis=1)
        keys = self.keys[:, lanes]
        zero = jnp.zeros_like(keys)
        lane = lax.broadcasted_iota(jnp.int32, (LINE, HALF), 1) // HEAD
        for head in range(IN_GROUP):
            head_keys = jnp.where(lane == head, keys, zero)
            head_keys = jnp.concatenate([head_keys, head_keys], axis=1)
            for start in range(0, LINE, BLOCK):
                here = slice(start, start + BLOCK)
                for chunk in range(0, LINE, self.chunk):
                    rows = slice(chunk, chunk + self.chunk)
                    scores = dot(head_keys[rows], query[here], 1, 1)
                    if self.shift:
                        largest = jnp.max(scores, axis=0, keepdims=True)
                        self.largest[group, head, chunk, start] = largest
                        scores = scores - largest
                    weights = jnp.exp2(scores).astype(jnp.bfloat16)
                    self.probs[group * IN_GROUP + head, rows, here] = weights

    def mix(self, group):
        ones = jnp.ones((16, LINE), jnp.bfloat16)
        for head in range(IN_GROUP):
            index = group * IN_GROUP + head
            values = jnp.concatenate([self.values[index * HEAD : (index + 1) * HEAD], ones], axis=0)
            if self.shift:
                total = self.sum_chunks(group, head, values)
            else:
                total = matmul(values, self.probs[index])
                weight = total[HEAD : HEAD + 1]
                fits = (weight >= LEAST) & (weight <= MOST)
                self.fits.append(jnp.where(fits, 1.0, 0.0))
            self.mixed.append((total[:HEAD] * (1.0 / total[HEAD : HEAD + 1])).astype(jnp.bfloat16))

    def sum_chunks(self, group, head, values):
        chunks = range(0, LINE, self.chunk)
        scales = [
            jnp.concatenate(
                [self.largest[group, head, chunk, start] for start in range(0, LINE, BLOCK)], axis=1
            )
            for chunk in chunks
        ]
        largest = functools.reduce(jnp.maximum, scales)
        total = 0.0
        for chunk, scale in zip(chunks, scales):
            rows = slice(chunk, chunk + self.chunk)
            part = matmul(values[:, rows], self.probs[group * IN_GROUP + head, rows])
            total += part * jnp.exp2(scale - largest)
        return total

    def finish(self):
        self.store(self.load() + dot(jnp.concatenate(self.mixed, axis=0), self.out_w[...], 0, 0))


def run(lines):
    lines[0].project()
    lines[0].weigh(0)
    for line, later in zip(lines, lines[1:] + [None]):
        line.mix(0)
        line.weigh(1)
        if later is not None:
            later.project()
        line.mix(1)
        if later is not None:
            later.weigh(0)
        line.finish()


def attend(make):
    lines = [make(False, j) for j in range(LINES)]
    run(lines)
    fits = functools.reduce(jnp.minimum, [part for line in lines for part in line.fits])

    @pl.when(jnp.min(fits) < 0.5)
    def _():
        def again(j, carry):
            run([make(True, j)])
            return carry

        lax.fori_loop(0, LINES, again, 0)


def pick(first, left, right):
    if isinstance(first, bool):
        return left if first else right
    return jnp.where(first, left, right)


def row_kernel(cells, gains, qk_w, val_w, out_w, out, later_out, last_out, probs, turned):
    gain = gains.at[0:1]
    later_out[...] = gains[1:2]
    last_out[...] = gains[2:3]

    def line(shift, j):
        def load():
            return cells[:, j].reshape(LINE, WIDTH).astype(jnp.float32)

        def store(done):
            for lanes in range(GROUPS):
                turned[lanes, pl.ds(j, LINE, stride=LINES), :] = done[:, lanes * HALF : (lanes + 1) * HALF]

        return Line(shift, load, store, gain, qk_w, val_w, out_w, probs)

    attend(line)
    n_row, n_col, deep = out.shape[:3]
    for lanes in range(GROUPS):
        here = slice(lanes * HALF, (lanes + 1) * HALF)
        blocks = turned[lanes].astype(jnp.bfloat16).reshape(n_col, n_row, deep, HALF)
        for r in range(n_row):
            out[r, :, :, here] = blocks[:, r]


def col_kernel(cells, gain, qk_w, val_w, out_w, out, probs):

    def line(shift, m):
        def load():
            tiles = cells[...].reshape(LINE // LINES, LINES * LINES, WIDTH).astype(jnp.float32)
            tiles = pick(m < 2, tiles[:, :8], tiles[:, 8:]).reshape(LINE // 8, 2, 8, WIDTH)
            even, odd = tiles[:, 0], tiles[:, 1]
            first = m % 2 == 0
            even = pick(first, even, pltpu.roll(even, LINES, 1))
            odd = pick(first, pltpu.roll(odd, LINES, 1), odd)
            row = lax.broadcasted_iota(jnp.int32, even.shape, 1)
            return jnp.where(row < LINES, even, odd).reshape(LINE, WIDTH)

        def store(done):
            out[:, m] = done.astype(jnp.bfloat16).reshape(out.shape[0], out.shape[2], WIDTH)

        return Line(shift, load, store, gain, qk_w, val_w, out_w, probs)

    attend(line)


def mlp_kernel(blocks, gain, in_w, out_w, out, swap, done, sems):
    rows, cols = out.shape[:2]
    deep = rows // LINES
    cells = deep * cols
    to = lax.broadcasted_iota(jnp.int32, (cells, cells), 0)
    come = lax.broadcasted_iota(jnp.int32, (cells, cells), 1)
    moved = come == to % cols * deep + to // cols
    swap[...] = jnp.where(moved, 1.0, 0.0).astype(jnp.bfloat16)
    parts = [slice(part * deep, (part + 1) * deep) for part in range(LINES)]
    lines = [matmul(swap[...], blocks[:, :, here].reshape(cells, WIDTH)) for here in parts]
    normed = [layer_norm(line, gain[...]).astype(jnp.bfloat16) for line in lines]
    copies = []

    def widen(part):
        pre = matmul(normed[part], in_w[...])
        inner = jnp.tanh(pre * (GELU_A + GELU_B * (pre * pre)))
        return (pre * (0.5 + 0.5 * inner)).astype(jnp.bfloat16)

    hidden = widen(0)
    for part, here in enumerate(parts):
        later = widen(part + 1) if part + 1 < LINES else None
        result = lines[part] + matmul(hidden, out_w[...])
        done[here] = result.astype(jnp.bfloat16).reshape(deep, cols, WIDTH)
        copies.append(pltpu.make_async_copy(done.at[here], out.at[here], sems.at[part]))
        copies[-1].start()
        hidden = later
    for copy in copies:
        copy.wait()


IN_VMEM = pl.BlockSpec(memory_space=pltpu.VMEM)
PARAMS = pltpu.CompilerParams(vmem_limit_bytes=40 * 2**20)


def bf16(*shape):
    return jax.ShapeDtypeStruct(shape, jnp.bfloat16)


def attend_scratch():
    return [pltpu.VMEM((HEADS, LINE, LINE), jnp.bfloat16)]


def row_attention(n_row, strips, gains, qk_w, val_w, out_w):
    n_col = strips.shape[0]
    return pl.pallas_call(
        row_kernel,
        in_specs=[IN_VMEM] * 5,
        out_specs=[IN_VMEM] * 3,
        out_shape=[bf16(n_row, n_col, LINES * LINES, WIDTH)]
        + [jax.ShapeDtypeStruct((1, WIDTH), jnp.float32)] * 2,
        scratch_shapes=attend_scratch() + [pltpu.VMEM((GROUPS, LINES * LINE, HALF), jnp.float32)],
        compiler_params=PARAMS,
        name="row_attention",
    )(strips, gains, qk_w, val_w, out_w)


def col_attention(n_row, columns, *weights):
    return pl.pallas_call(
        col_kernel,
        in_specs=[IN_VMEM] * 5,
        out_specs=IN_VMEM,
        out_shape=bf16(n_row, LINES, LINE // n_row, WIDTH),
        scratch_shapes=attend_scratch(),
        compiler_params=PARAMS,
        name="col_attention",
    )(columns, *weights)


def mlp(cols, blocks, *weights):
    rows = blocks.shape[2]
    cells = rows // LINES * cols
    return pl.pallas_call(
        mlp_kernel,
        in_specs=[IN_VMEM] * 4,
        out_specs=pl.BlockSpec(memory_space=pl.ANY),
        out_shape=bf16(rows, cols, WIDTH),
        scratch_shapes=[
            pltpu.VMEM((cells, cells), jnp.bfloat16),
            pltpu.VMEM((rows, cols, WIDTH), jnp.bfloat16),
            pltpu.SemaphoreType.DMA((LINES,)),
        ],
        compiler_params=PARAMS,
        name="mlp",
    )(blocks, *weights)


def per_device(
    cells,
    row_gain,
    row_qk,
    row_value,
    row_out,
    col_gain,
    col_qk,
    col_value,
    col_out,
    mlp_gain,
    mlp_in,
    mlp_out,
):
    n_row = lax.axis_size("row")
    n_col = lax.axis_size("col")
    rows, cols, width = cells.shape
    gains = jnp.stack([row_gain, col_gain, mlp_gain])
    strips = lax.all_to_all(cells, "col", split_axis=0, concat_axis=0, tiled=True)
    strips = strips.reshape(n_col, LINES, cols, width)
    after_rows, col_gain, mlp_gain = row_attention(n_row, strips, gains, row_qk, row_value, row_out)
    columns = lax.all_to_all(
        after_rows.reshape(-1, width), ("row", "col"), split_axis=0, concat_axis=0, tiled=True
    )
    after_cols = col_attention(n_row, columns, col_gain, col_qk, col_value, col_out)
    blocks = lax.all_to_all(
        after_cols.reshape(-1, width), "row", split_axis=0, concat_axis=0, tiled=True
    )
    return mlp(cols, blocks.reshape(n_row, LINES, rows, width), mlp_gain, mlp_in, mlp_out)


def solution(mesh):
    in_specs = (P("row", "col", None), P(), P(), P(), P(), P(), P(), P(), P(), P(), P(), P())
    out_specs = P("row", "col", None)
    return jax.shard_map(
        per_device, mesh=mesh, in_specs=in_specs, out_specs=out_specs, check_vma=False
    )
```
